256 devices in a mesh: node: 16 (over y, x_hi, core), cross: 16 (over x_lo, z).
Axes of the slice: x: 4 (x_hi: 2, x_lo: 2; x = x_hi * 2 + x_lo), y: 4, z: 8, core: 2. Of those that a mesh axis runs over, the one named last changes fastest.
Arguments:
- activations: bfloat16 [65536, 8192], P(('node', 'cross')), may hold values from -24 to 24
- queries: bfloat16 [65536, 4096], P(('node', 'cross')), may hold values from -150 to 150
- keys: bfloat16 [65536, 512], P(('node', 'cross')), may hold values from -6 to 6
- segment_ids: int32 [256, 256], P(('node', 'cross')), may hold values from 0 to 3, never falling along the last dimension, each value on 1 to 128 neighbouring positions
- cotangent: bfloat16 [65536, 4096], P(('node', 'cross')), may hold values from -6 to 6
- value_codes: bfloat16 [8192, 512], P(('node', 'cross')), may hold values from -127 to 127
- value_scales: float32 [8192, 4], P(('node', 'cross')), may hold values from 5e-05 to 0.00045
Outputs:
- attended: bfloat16 [65536, 4096], P(('node', 'cross'))
- weight_grad: float32 [8192, 512], P(('node', 'cross'))
The draws below stay inside these ranges and needn't reach their ends.
All inputs are finite; a program needn't handle non-finite values.
Results may differ from the reference program's by a relative error of at most 0.017.
Values may be sent and summed in bfloat16 or wider, within the bound.
No kernel may reach another device: no remote copies, remote signals or barrier semaphores. Data moves between devices by JAX's collectives and lax.ppermute only.
A program may use at most 128 MiB of HBM per device.

```python
import math
import jax
import jax.numpy as jnp
import numpy as np
from jax import lax

D = 8192
HEAD_DIM = 128
HEADS = 32
KV_HEADS = 4
TOK_DEV = 256
SEGMENTS = 4
GROUP = 8
VW = 512
QW = 4096
TOKENS = 65536
DEVICES = 256


def shared_keys(key):
    base = jax.random.normal(key, (TOKENS, KV_HEADS, HEAD_DIM), jnp.float32)
    return jnp.clip(base, -6.0, 6.0)


def draw_keys(key, part):
    base = shared_keys(key)
    return base.reshape(TOKENS, VW).astype(jnp.bfloat16)


def draw_queries(key, part):
    key = jax.random.fold_in(key, 23)
    noise = jnp.clip(jax.random.normal(key, (TOKENS, HEADS, HEAD_DIM), jnp.float32), -6.0, 6.0)
    return noise.reshape(TOKENS, QW).astype(jnp.bfloat16)


def raised(values, stream_key, source, target, shards_of, factor):
    def block_of(dim):
        return (jnp.arange(values.shape[dim]) // (values.shape[dim] // shards_of)).reshape((-1,) + (1,) * (values.ndim - 1 - dim))

    one_side = jax.random.permutation(stream_key, shards_of)[block_of(target)]
    second = (block_of(target) + shards_of // 2) % shards_of
    return jnp.where((block_of(source) == one_side) | (block_of(source) == second), factor * values, values)


def steps_of(rng, dims, cuts, smallest, top_value):
    factor_of, own = 1.0, jax.random.fold_in(rng, 6)
    for dim, shards_of in cuts:
        draws = jnp.exp(jax.random.uniform(jax.random.fold_in(own, dim), (shards_of,), jnp.float32, smallest / len(cuts), top_value / len(cuts)))
        factor_of = factor_of * jnp.repeat(draws, dims[dim] // shards_of).reshape([-1 if axis == dim else 1 for axis in range(len(dims))])
    return factor_of


def profile(amount, total, reach, skew):
    portions = [(1 << 20) // math.isqrt(standing ** skew) + 1 for standing in range(2, amount + 1)]
    spare, given = total - reach - (amount - 1), [1] * (amount - 1)
    while spare > 0:
        movable = [i for i in range(amount - 1) if given[i] < reach]
        mass, remaining = sum([portions[i] for i in movable]), spare
        for i in movable:
            addition = min(reach - given[i], max(1, remaining * portions[i] // mass), spare)
            given[i] = given[i] + addition
            spare = spare - addition
    return np.array([reach] + given)


def uneven(rng, count, total, bound, skew):
    if count == 2:
        one = jax.random.randint(rng, (), max(1, total - bound), min(bound, total - 1) + 1)
        return jnp.stack([one, total - one])
    sizes = jnp.asarray(profile(count, total, bound, skew), jnp.int32)
    pairs = (count - 1) // 2
    donor, taker = sizes[1:1 + 2 * pairs:2], sizes[2:2 + 2 * pairs:2]
    slack = jnp.minimum(donor - 1, bound - taker)
    shifted = jax.random.randint(jax.random.fold_in(rng, 1), (pairs,), 0, 1 << 20) % (slack + 1)
    sizes = sizes.at[1:1 + 2 * pairs:2].set(donor - shifted).at[2:2 + 2 * pairs:2].set(taker + shifted)
    return sizes[jax.random.permutation(jax.random.fold_in(rng, 2), count)]


def normal_values(own_key, shape, deviation, reach, split=(), held_as=jnp.bfloat16):
    values = jax.random.normal(own_key, shape, jnp.float32) * deviation
    if len(split) > 0:
        values = steps_of(own_key, shape, split, -0.22, 0.18) * values
    return jnp.clip(values, min=-reach, max=reach).astype(held_as)


def noise_with(key, dims, spread, limit, split, heavy, held_as=jnp.bfloat16):
    values = spread * jax.random.normal(key, dims, jnp.float32)
    if split:
        values = values * steps_of(key, dims, split, -0.22, 0.18)
    return jnp.clip(raised(values, jax.random.fold_in(key, 3), *heavy), -limit, limit).astype(held_as)


def setup_inputs(seed: int = 0) -> dict:
    arg_keys = jax.random.split(jax.random.key(seed), 8)
    return {
        "activations": noise_with(arg_keys[0], (TOKENS, D), 1.0, 24.0, ((0, 256),), (0, 1, 256, 6.0)),
        "queries": draw_queries(jax.random.fold_in(arg_keys[7], 71), 0),
        "keys": draw_keys(jax.random.fold_in(arg_keys[7], 71), 0),
        "segment_ids": jax.vmap(lambda own: jnp.searchsorted(jnp.cumsum(uneven(own, SEGMENTS, TOK_DEV, TOK_DEV // 2, 2)), jnp.arange(TOK_DEV), side="right"))(jax.random.split(arg_keys[3], DEVICES)).reshape((DEVICES, TOK_DEV)).astype(jnp.int32),
        "cotangent": normal_values(arg_keys[4], (TOKENS, QW), 1.0, 6.0, ((0, 256),)),
        "value_codes": jnp.clip(jax.random.uniform(arg_keys[5], (D, VW), jnp.float32, -127.0, 127.0) * steps_of(arg_keys[5], (D, VW), ((0, 256),), -0.4, 0.0), -127.0, 127.0).astype(jnp.bfloat16),
        "value_scales": jnp.clip(jnp.exp(math.log(0.00045) - 2.1972246 * jax.random.uniform(arg_keys[6], (D, KV_HEADS), jnp.float32) ** steps_of(arg_keys[6], (D, KV_HEADS), ((0, 256),), -0.2, 0.2)), 4.999999873689376e-05, 0.00045),
    }


def attention_weights(query_rows, key_rows, segment):
    length = query_rows.shape[0]
    query_f = query_rows.astype(jnp.float32).reshape(length, KV_HEADS, GROUP, HEAD_DIM)
    key_f = key_rows.astype(jnp.float32).reshape(length, KV_HEADS, HEAD_DIM)
    scores = jnp.einsum('tgcd,sgd->gcts', query_f, key_f) / math.sqrt(HEAD_DIM)
    position = jnp.arange(length)
    allowed = (position[None, :] <= position[:, None]) & (segment[:, None] == segment[None, :])
    scores = jnp.where(allowed, scores, -1e+30)
    highest = lax.optimization_barrier(jnp.max(scores, axis=-1, keepdims=True))
    exponent = jnp.exp(scores - highest)
    return (exponent / lax.optimization_barrier(jnp.sum(exponent, axis=-1, keepdims=True))).astype(jnp.bfloat16)

def reference(activations, queries, keys, segment_ids, cotangent, value_codes, value_scales):
    weight = (value_codes.astype(jnp.float32).reshape(D, KV_HEADS, HEAD_DIM) * value_scales[:, :, None]).reshape(D, VW).astype(jnp.bfloat16)
    values = jnp.dot(activations, weight, preferred_element_type=jnp.float32).astype(jnp.bfloat16)

    def per_sequence(inputs):
        query_rows, key_rows, value_rows, segment, grad_rows = inputs
        probability = attention_weights(query_rows, key_rows, segment).astype(jnp.float32)
        value_f = value_rows.astype(jnp.float32).reshape(TOK_DEV, KV_HEADS, HEAD_DIM)
        attended = jnp.einsum('gcts,sgd->tgcd', probability, value_f).reshape(TOK_DEV, QW).astype(jnp.bfloat16)
        grad_f = grad_rows.astype(jnp.float32).reshape(TOK_DEV, KV_HEADS, GROUP, HEAD_DIM)
        dvalue = jnp.einsum('gcts,tgcd->sgd', probability, grad_f).reshape(TOK_DEV, VW).astype(jnp.bfloat16)
        return (attended, dvalue)
    attended, dvalue = lax.map(per_sequence, (queries.reshape(DEVICES, TOK_DEV, QW), keys.reshape(DEVICES, TOK_DEV, VW), values.reshape(DEVICES, TOK_DEV, VW), segment_ids, cotangent.reshape(DEVICES, TOK_DEV, QW)))
    attended = attended.reshape(TOKENS, QW)
    dvalue = dvalue.reshape(TOKENS, VW)
    weight_grad = jnp.dot(activations.T, dvalue, preferred_element_type=jnp.float32) * (1.0 / math.sqrt(TOKENS))
    return (attended, weight_grad)
```

```python
import functools
import math

import jax
import jax.numpy as jnp
from jax import lax
from jax.experimental import pallas as pl
from jax.experimental.pallas import tpu as pltpu
from jax.sharding import Mesh, PartitionSpec as P

NY, NX, NC, NZ = 4, 4, 2, 8
AXES = ("y", "xh", "c", "xl", "z")
BF, F32 = jnp.bfloat16, jnp.float32
VMEM = 60 * 1024 * 1024


def device_index(y, x, c, z):
    return (((y * 2 + x // 2) * 2 + c) * 2 + x % 2) * NZ + z


def permute(array, move):
    pairs = []
    for y in range(NY):
        for x in range(NX):
            for c in range(NC):
                for z in range(NZ):
                    ty, tx, tc, tz = move(y, x, c, z)
                    pairs.append(
                        (device_index(y, x, c, z), device_index(ty % NY, tx % NX, tc, tz % NZ))
                    )
    return lax.ppermute(array, AXES, pairs)


def along_y(array):
    return permute(array, lambda y, x, c, z: (y + 1 - 2 * c, x, c, z))


def along_x(array):
    return permute(array, lambda y, x, c, z: (y, x + 1 - 2 * c, c, z))


def along_z(array, k):
    return permute(array, lambda y, x, c, z: (y, x, c, z + k))


def swap_cores(array):
    return permute(array, lambda y, x, c, z: (y, x, 1 - c, z))


def params(**more):
    return pltpu.CompilerParams(vmem_limit_bytes=VMEM, **more)


def pick_kernel(place, act_ref, out_ref):
    out_ref[...] = act_ref[...]


def other_half(place, activations):
    tokens, width = activations.shape
    blocks = width // 1024
    return pl.pallas_call(
        pick_kernel,
        out_shape=jax.ShapeDtypeStruct((tokens, width // 2), BF),
        grid_spec=pltpu.PrefetchScalarGridSpec(
            num_scalar_prefetch=1,
            grid=(blocks,),
            in_specs=[pl.BlockSpec((tokens, 512), lambda i, p: (0, 2 * i + 1 - p[2]))],
            out_specs=pl.BlockSpec((tokens, 512), lambda i, p: (0, i)),
        ),
        compiler_params=params(),
        name="other_half",
    )(place, activations)


def weights_kernel(group, head_dim, q_ref, k_ref, cot_ref, row_ref, col_ref, p_ref, dv_ref, bias):
    length = q_ref.shape[0]

    @pl.when(pl.program_id(0) == 0)
    def _():
        u = lax.broadcasted_iota(jnp.int32, (length, length), 0)
        t = lax.broadcasted_iota(jnp.int32, (length, length), 1)
        allowed = (u <= t) & (col_ref[...] == row_ref[...])
        bias[...] = jnp.where(allowed, 0.0, -1e30)

    rate = math.log2(math.e) / math.sqrt(head_dim)
    total = jnp.zeros((length, head_dim), F32)
    for h in range(group):
        cols = slice(h * head_dim, (h + 1) * head_dim)
        scores = lax.dot_general(
            k_ref[...], q_ref[:, cols], (((1,), (1,)), ((), ())), preferred_element_type=F32
        )
        scores = scores + bias[...]
        highest = jnp.max(scores, axis=0, keepdims=True)
        exponent = jnp.exp2((scores - highest) * rate)
        share = 1.0 / jnp.sum(exponent, axis=0, keepdims=True)
        probability = (exponent * share).astype(BF)
        p_ref[h] = probability
        total = total + jnp.dot(probability, cot_ref[:, cols], preferred_element_type=F32)
    dv_ref[...] = total.astype(BF)


def attention_weights(queries, keys, segment_ids, cotangent, kv_heads):
    length, width = queries.shape
    head_dim = keys.shape[1] // kv_heads
    group = width // keys.shape[1]
    wide = group * head_dim
    return pl.pallas_call(
        functools.partial(weights_kernel, group, head_dim),
        out_shape=(
            jax.ShapeDtypeStruct((kv_heads * group, length, length), BF),
            jax.ShapeDtypeStruct((length, kv_heads * head_dim), BF),
        ),
        grid=(kv_heads,),
        in_specs=[
            pl.BlockSpec((length, wide), lambda g: (0, g)),
            pl.BlockSpec((length, head_dim), lambda g: (0, g)),
            pl.BlockSpec((length, wide), lambda g: (0, g)),
            pl.BlockSpec((1, length), lambda g: (0, 0)),
            pl.BlockSpec((length, 1), lambda g: (0, 0)),
        ],
        out_specs=(
            pl.BlockSpec((group, length, length), lambda g: (g, 0, 0)),
            pl.BlockSpec((length, head_dim), lambda g: (0, g)),
        ),
        scratch_shapes=[pltpu.VMEM((length, length), F32)],
        compiler_params=params(),
        cost_estimate=pl.CostEstimate(
            flops=4 * width * length * length,
            bytes_accessed=8 * 1024 * 1024,
            transcendentals=kv_heads * group * length * length,
        ),
        name="attention_weights",
    )(queries, keys, cotangent, segment_ids, segment_ids.reshape(length, 1))


def product_kernel(factor, place, own_ref, got_ref, dvo_ref, dvg_ref, a_ref, b_ref):
    x, c = place[1], place[2]
    step = 1 - 2 * c
    first = (((0,), (0,)), ((), ()))
    for j in range(NX):
        xj = (x - j * step + NX) % NX
        at_own = pl.multiple_of((xj // 2) * 1024 + c * 512 + (xj % 2) * 256, 256)
        at_got = pl.multiple_of(xj * 256, 256)
        rows = lax.dot_general(
            own_ref[:, pl.ds(at_own, 256)], dvo_ref[...], first, preferred_element_type=F32
        ) + lax.dot_general(
            got_ref[:, pl.ds(at_got, 256)], dvg_ref[...], first, preferred_element_type=F32
        )
        rows = (rows * factor).astype(BF)
        a_ref[0, j] = rows[:, :256]
        b_ref[j, 0] = rows[:, 256:]


def product(place, act_own, act_got, dv_own, dv_got, factor):
    tokens, width = act_own.shape

    def row(k, p):
        return (p[0] - k * (1 - 2 * p[2]) + NY) % NY

    shape = jax.ShapeDtypeStruct((4, 4, 256, 256), BF)
    return pl.pallas_call(
        functools.partial(product_kernel, factor),
        out_shape=(shape, shape),
        grid_spec=pltpu.PrefetchScalarGridSpec(
            num_scalar_prefetch=1,
            grid=(NY,),
            in_specs=[
                pl.BlockSpec((tokens, width // NY), lambda k, p: (0, row(k, p))),
                pl.BlockSpec((tokens, width // NY // 2), lambda k, p: (0, row(k, p))),
                pl.BlockSpec((tokens, 512), lambda k, p: (0, 0)),
                pl.BlockSpec((tokens, 512), lambda k, p: (0, 0)),
            ],
            out_specs=(
                pl.BlockSpec((1, 4, 256, 256), lambda k, p: (k, 0, 0, 0)),
                pl.BlockSpec((4, 1, 256, 256), lambda k, p: (0, k, 0, 0)),
            ),
        ),
        compiler_params=params(),
        cost_estimate=pl.CostEstimate(
            flops=2 * tokens * width * 512, bytes_accessed=10 * 1024 * 1024, transcendentals=0
        ),
        name="product",
    )(place, act_own, act_got, dv_own, dv_got)


def order_kernel(place, *refs):
    pieces, (a_ref, b_ref) = refs[:NZ], refs[NZ:]
    z = place[3]
    for k in range(NZ):
        at = pl.ds(pl.multiple_of(((z - k + NZ) % NZ) * 32, 32), 32)
        a_ref[at, :] = pieces[k][:, :256]
        b_ref[at, :] = pieces[k][:, 256:]


def order_rows(place, pieces):
    shape = jax.ShapeDtypeStruct((256, 256), BF)
    return pl.pallas_call(
        order_kernel,
        out_shape=(shape, shape),
        in_specs=[pl.BlockSpec(memory_space=pltpu.SMEM)]
        + [pl.BlockSpec(memory_space=pltpu.VMEM)] * NZ,
        out_specs=(pl.BlockSpec(memory_space=pltpu.VMEM),) * 2,
        compiler_params=params(),
        name="order_rows",
    )(place, *pieces)


def spread_kernel(place, ra_ref, oa_ref, rb_ref, ob_ref, *outs):
    z = place[3]
    for k in range(NZ):
        at = pl.ds(pl.multiple_of(((z + k) % NZ) * 32, 32), 32)
        a = ra_ref[at, :].astype(F32) + oa_ref[at, :].astype(F32)
        b = rb_ref[at, :].astype(F32) + ob_ref[at, :].astype(F32)
        outs[k][:, :256] = a.astype(outs[k].dtype)
        outs[k][:, 256:] = b.astype(outs[k].dtype)


def spread_rows(place, got_a, own_a, got_b, own_b):
    return pl.pallas_call(
        spread_kernel,
        out_shape=tuple(
            jax.ShapeDtypeStruct((32, 512), F32 if k == 0 else BF) for k in range(NZ)
        ),
        in_specs=[pl.BlockSpec(memory_space=pltpu.SMEM)]
        + [pl.BlockSpec(memory_space=pltpu.VMEM)] * 4,
        out_specs=(pl.BlockSpec(memory_space=pltpu.VMEM),) * NZ,
        compiler_params=params(),
        name="spread_rows",
    )(place, got_a, own_a, got_b, own_b)


def values_kernel(place, own_ref, got_ref, *refs):
    a_refs, b_refs = refs[:8], refs[8:16]
    vo_ref, vg_ref = refs[16:]
    y, x, c = place[0], place[1], place[2]
    step = 1 - 2 * c
    own = [jnp.zeros((256, 256), F32)] * 2
    got = [jnp.zeros((256, 256), F32)] * 2
    for k in range(NY):
        yk = (y - k * step + NY) % NY
        for j in range(NX):
            xj = (x - j * step + NX) % NX
            at_got = pl.multiple_of((yk * 4 + xj) * 256, 256)
            at_own = pl.multiple_of(yk * 2048 + (xj // 2) * 1024 + c * 512 + (xj % 2) * 256, 256)
            left = own_ref[:, pl.ds(at_own, 256)]
            right = got_ref[:, pl.ds(at_got, 256)]
            for i, w in enumerate((a_refs[2 * k + j // 2][j % 2], b_refs[2 * j + k // 2][k % 2])):
                own[i] = own[i] + jnp.dot(left, w, preferred_element_type=F32)
                got[i] = got[i] + jnp.dot(right, w, preferred_element_type=F32)
    for i in range(2):
        vo_ref[:, i * 256 : (i + 1) * 256] = own[i]
        vg_ref[:, i * 256 : (i + 1) * 256] = got[i]


def partial_values(place, act_own, act_got, a_pieces, b_pieces):
    shape = jax.ShapeDtypeStruct((act_own.shape[0], 512), F32)
    return pl.pallas_call(
        values_kernel,
        out_shape=(shape, shape),
        in_specs=[pl.BlockSpec(memory_space=pltpu.SMEM)]
        + [pl.BlockSpec(memory_space=pltpu.VMEM)] * 18,
        out_specs=(pl.BlockSpec(memory_space=pltpu.VMEM),) * 2,
        compiler_params=params(),
        cost_estimate=pl.CostEstimate(
            flops=2 * 256 * 8192 * 512, bytes_accessed=11 * 1024 * 1024, transcendentals=0
        ),
        name="partial_values",
    )(place, act_own, act_got, *a_pieces, *b_pieces)


def attend_kernel(group, head_dim, p_ref, vo_ref, vg_ref, out_ref):
    values = (vo_ref[...] + vg_ref[...]).astype(BF)
    for h in range(group):
        out_ref[:, h * head_dim : (h + 1) * head_dim] = lax.dot_general(
            p_ref[h], values, (((0,), (0,)), ((), ())), preferred_element_type=F32
        ).astype(BF)


def attend(probability, values_own, values_got, kv_heads):
    heads, length, _ = probability.shape
    head_dim = values_own.shape[1] // kv_heads
    group = heads // kv_heads
    return pl.pallas_call(
        functools.partial(attend_kernel, group, head_dim),
        out_shape=jax.ShapeDtypeStruct((length, heads * head_dim), BF),
        grid=(kv_heads,),
        in_specs=[
            pl.BlockSpec((group, length, length), lambda g: (g, 0, 0)),
            pl.BlockSpec((length, head_dim), lambda g: (0, g)),
            pl.BlockSpec((length, head_dim), lambda g: (0, g)),
        ],
        out_specs=pl.BlockSpec((length, group * head_dim), lambda g: (0, g)),
        compiler_params=params(),
        cost_estimate=pl.CostEstimate(
            flops=2 * heads * head_dim * length * length,
            bytes_accessed=7 * 1024 * 1024,
            transcendentals=0,
        ),
        name="attend",
    )(probability, values_own, values_got)


def ring_gather(move, block):
    held = [block]
    for _ in range(3):
        held.append(move(held[-1]))
    return held


def gather(place, weight):
    pieces = [weight] + [along_z(weight, k) for k in range(1, NZ)]
    a, b = order_rows(place, pieces)
    a_near, b_near = ring_gather(along_x, a), ring_gather(along_y, b)
    a_all = [None] * 8
    b_all = [None] * 8
    for half in range(2):
        for k, block in enumerate(ring_gather(along_y, jnp.stack(a_near[2 * half : 2 * half + 2]))):
            a_all[2 * k + half] = block
        for k, block in enumerate(ring_gather(along_x, jnp.stack(b_near[2 * half : 2 * half + 2]))):
            b_all[2 * k + half] = block
    return a_all, b_all


def add(left, right):
    return (left.astype(F32) + right.astype(F32)).astype(BF)


def ring_sum(move, chunks):
    travel = chunks[1]
    for k in (2, 3):
        travel = add(move(travel), chunks[k])
    return move(travel)


def reduce_two(first, second, parts):
    halves = []
    for half in range(2):
        chunks = [parts[k, 2 * half : 2 * half + 2] for k in range(4)]
        halves.append(add(ring_sum(first, chunks), chunks[0]))
    blocks = [halves[0][0], halves[0][1], halves[1][0], halves[1][1]]
    return ring_sum(second, blocks), blocks[0]


def reduce(place, a_parts, b_parts):
    got_a, own_a = reduce_two(along_y, along_x, a_parts)
    got_b, own_b = reduce_two(along_x, along_y, b_parts)
    rows = spread_rows(place, got_a, own_a, got_b, own_b)
    total = rows[0]
    for k in range(1, NZ):
        total = total + along_z(rows[k], k).astype(F32)
    return total


def local(activations, queries, keys, segment_ids, cotangent, value_codes, value_scales):
    rows_here, kv_heads = value_scales.shape
    x = lax.axis_index("xh") * 2 + lax.axis_index("xl")
    place = jnp.stack(
        [lax.axis_index("y"), x, lax.axis_index("c"), lax.axis_index("z")]
    ).astype(jnp.int32)
    weight = (
        value_codes.astype(F32).reshape(rows_here, kv_heads, -1) * value_scales[:, :, None]
    ).reshape(rows_here, -1).astype(BF)
    act_got = swap_cores(other_half(place, activations))
    a_pieces, b_pieces = gather(place, weight)
    probability, dvalue = attention_weights(queries, keys, segment_ids, cotangent, kv_heads)
    factor = 1.0 / math.sqrt(activations.shape[0] * NY * NX * NC * NZ)
    a_parts, b_parts = product(
        place, activations, act_got, dvalue, swap_cores(dvalue), factor
    )
    weight_grad = reduce(place, a_parts, b_parts)
    values_own, values_other = partial_values(place, activations, act_got, a_pieces, b_pieces)
    attended = attend(probability, values_own, swap_cores(values_other), kv_heads)
    return (attended, weight_grad)


def solution(mesh):
    inner = Mesh(mesh.devices.reshape(NY, 2, NC, 2, NZ), AXES)
    rows = P(AXES, None)
    return jax.shard_map(
        local, mesh=inner, in_specs=(rows,) * 7, out_specs=(rows, rows), check_vma=False
    )
```

```python
import functools
import math

import jax
import jax.numpy as jnp
from jax import lax
from jax.experimental import pallas as pl
from jax.experimental.pallas import tpu as pltpu
from jax.sharding import Mesh, PartitionSpec as P

NY, NX, NC, NZ = 4, 4, 2, 8
AXES = ("y", "xh", "c", "xl", "z")
BF, F32 = jnp.bfloat16, jnp.float32
MIB = 1024 * 1024


def swap_cores(array):
    return lax.ppermute(array, "c", [(0, 1), (1, 0)])


def params(mib=20):
    return pltpu.CompilerParams(vmem_limit_bytes=mib * MIB)


def pick_kernel(place, act_ref, out_ref, sems):
    blocks = out_ref.shape[1] // 512
    copies = []
    for i in range(blocks):
        at = pl.multiple_of(i * 1024 + (1 - place[0]) * 512, 512)
        copies.append(
            pltpu.make_async_copy(
                act_ref.at[:, pl.ds(at, 512)], out_ref.at[:, pl.ds(i * 512, 512)], sems.at[i]
            )
        )
    for copy in copies:
        copy.start()
    for copy in copies:
        copy.wait()


def other_half(place, activations):
    tokens, width = activations.shape
    return pl.pallas_call(
        pick_kernel,
        out_shape=jax.ShapeDtypeStruct((tokens, width // 2), BF),
        in_specs=[pl.BlockSpec(memory_space=pltpu.SMEM), pl.BlockSpec(memory_space=pltpu.HBM)],
        out_specs=pl.BlockSpec(memory_space=pltpu.VMEM),
        scratch_shapes=[pltpu.SemaphoreType.DMA((width // 1024,))],
        compiler_params=params(60),
        cost_estimate=pl.CostEstimate(flops=0, bytes_accessed=2 * tokens * width, transcendentals=0),
        name="other_half",
    )(place, activations)


def copies_of(pairs, sems):
    return [pltpu.make_async_copy(a, b, sems.at[i]) for i, (a, b) in enumerate(pairs)]


def start(copies):
    for copy in copies:
        copy.start()


def columns(ref, i, width):
    return ref.at[:, pl.ds(i * width, width)]


def weights_kernel(head_dim, q_ref, k_ref, cot_ref, segment_ref, p_ref, dv_ref):
    length = q_ref.shape[0]
    kv_heads = k_ref.shape[1] // head_dim
    group = q_ref.shape[1] // k_ref.shape[1]
    row = segment_ref[...]
    column = jnp.broadcast_to(row.astype(F32), (128, length)).T[:, :1].astype(jnp.int32)
    u = lax.broadcasted_iota(jnp.int32, (length, length), 0)
    t = lax.broadcasted_iota(jnp.int32, (length, length), 1)
    bias = jnp.where((u <= t) & (column == row), 0.0, -1e30)
    rate = math.log2(math.e) / math.sqrt(head_dim)
    for g in range(kv_heads):
        total = jnp.zeros((length, head_dim), F32)
        own = slice(g * head_dim, (g + 1) * head_dim)
        for h in range(g * group, (g + 1) * group):
            cols = slice(h * head_dim, (h + 1) * head_dim)
            scores = lax.dot_general(
                k_ref[:, own], q_ref[:, cols], (((1,), (1,)), ((), ())), preferred_element_type=F32
            )
            scores = scores + bias
            highest = jnp.max(scores, axis=0, keepdims=True)
            exponent = jnp.exp2((scores - highest) * rate)
            share = 1.0 / jnp.sum(exponent, axis=0, keepdims=True)
            probability = (exponent * share).astype(BF)
            p_ref[h] = probability
            total = total + jnp.dot(probability, cot_ref[:, cols], preferred_element_type=F32)
        dv_ref[:, own] = total.astype(BF)


INSIDE = pl.BlockSpec(memory_space=pltpu.VMEM)
OUTSIDE = pl.BlockSpec(memory_space=pl.ANY)
HBM = pl.BlockSpec(memory_space=pltpu.HBM)
SCALARS = pl.BlockSpec(memory_space=pltpu.SMEM)


def cost(flops, mib, exps=0):
    return pl.CostEstimate(flops=flops, bytes_accessed=mib * MIB, transcendentals=exps)


def attention_weights(queries, keys, segment_ids, cotangent, kv_heads):
    length, width = queries.shape
    head_dim = keys.shape[1] // kv_heads
    heads = width // head_dim
    return pl.pallas_call(
        functools.partial(weights_kernel, head_dim),
        out_shape=(
            jax.ShapeDtypeStruct((heads, length, length), BF),
            jax.ShapeDtypeStruct(keys.shape, BF),
        ),
        in_specs=[INSIDE] * 4,
        out_specs=(INSIDE, INSIDE),
        compiler_params=params(),
        cost_estimate=cost(4 * width * length * length, 16, heads * length * length),
        name="attention_weights",
    )(queries, keys, cotangent, segment_ids)


def product_kernel(factor, place, own_ref, got_ref, dvo_ref, dvg_ref, *outs):
    c, y, x = place[0], place[2], place[3]
    dv_own = dvo_ref[...].astype(F32).T.astype(BF)
    dv_got = dvg_ref[...].astype(F32).T.astype(BF)
    for k in (1, 2, 3, 0):
        for m in range(4):
            ty = jnp.where(c == 0, (y + k) % 4, m)
            tx = jnp.where(c == 0, m, (x + k) % 4)
            at_own = pl.multiple_of((ty * 2 + tx // 2) * 1024 + c * 512 + (tx % 2) * 256, 256)
            at_got = pl.multiple_of((ty * 4 + tx) * 256, 256)
            rows = jnp.dot(
                dv_own, own_ref[:, pl.ds(at_own, 256)], preferred_element_type=F32
            ) + jnp.dot(dv_got, got_ref[:, pl.ds(at_got, 256)], preferred_element_type=F32)
            outs[k][m] = (rows * factor).astype(BF)


def product(place, act_own, act_got, dv_own, dv_got, factor):
    tokens, width = act_own.shape
    wide = dv_own.shape[1]
    return pl.pallas_call(
        functools.partial(product_kernel, factor),
        out_shape=(jax.ShapeDtypeStruct((4, wide, 256), BF),) * 4,
        in_specs=[SCALARS] + [INSIDE] * 4,
        out_specs=(INSIDE,) * 4,
        compiler_params=params(),
        cost_estimate=cost(2 * tokens * width * wide, 12),
        name="product",
    )(place, act_own, act_got, dv_own, dv_got)


def values_kernel(place, own_ref, got_ref, *refs):
    pieces, (vo_ref, vg_ref, weight, sw) = refs[: NZ + 1], refs[NZ + 1 :]
    rows, wide = pieces[0].shape[1:]
    c = place[0]
    places = weight.shape[0]
    spans = [(0, 0, places), (-1, 0, places), (1, 0, places), (-2, 0, places), (2, 0, places)]
    spans += [(-3, 0, places), (3, 0, places), (4, 0, places // 2), (4, places // 2, places // 2)]
    pairs = []
    for piece, (k, low, count) in zip(pieces, spans):
        z = (place[1] + k + NZ) % NZ
        at = pl.ds(pl.multiple_of(z * rows, rows), rows)
        pairs.append((piece, weight.at[pl.ds(low, count), at]))
    incoming = copies_of(pairs, sw)
    start(incoming)
    for copy in incoming:
        copy.wait()
    own = got = None
    for i in range(places // 2):
        at = pl.multiple_of(i * 1024 + c * 512, 512)
        block = weight[pl.ds(2 * i, 2)].reshape(512, wide)
        left = jnp.dot(own_ref[:, pl.ds(at, 512)], block, preferred_element_type=F32)
        right = jnp.dot(got_ref[:, i * 512 : (i + 1) * 512], block, preferred_element_type=F32)
        own, got = (left, right) if i == 0 else (own + left, got + right)
    vo_ref[...] = own
    vg_ref[...] = got


def partial_values(place, act_own, act_got, pieces):
    tokens, width = act_own.shape
    places, rows, wide = pieces[0].shape
    return pl.pallas_call(
        values_kernel,
        out_shape=(jax.ShapeDtypeStruct((tokens, wide), F32),) * 2,
        in_specs=[SCALARS, INSIDE, INSIDE] + [OUTSIDE] * (1 + NZ),
        out_specs=(INSIDE, INSIDE),
        scratch_shapes=[
            pltpu.VMEM((places, NZ * rows, wide), BF),
            pltpu.SemaphoreType.DMA((NZ + 1,)),
        ],
        compiler_params=params(),
        cost_estimate=cost(2 * tokens * width * wide, 12),
        name="partial_values",
    )(place, act_own, act_got, *pieces)


def add_kernel(place, *refs):
    sources, outs = refs[:4], refs[4:]
    near = jnp.where(place[0] == 0, place[3], place[2])
    for j in (1, 2, 3, 0):
        at = (near + j) % 4
        total = sources[0][at].astype(F32)
        for source in sources[1:]:
            total = total + source[at].astype(F32)
        outs[j][...] = total.astype(BF)


def add_far(place, parts):
    _, wide, rows = parts[0].shape
    return pl.pallas_call(
        add_kernel,
        out_shape=(jax.ShapeDtypeStruct((wide, rows), BF),) * 4,
        in_specs=[SCALARS] + [INSIDE] * 4,
        out_specs=(INSIDE,) * 4,
        compiler_params=params(),
        cost_estimate=cost(16 * rows * wide, 5),
        name="add_far",
    )(place, *parts)


def near_kernel(place, *refs):
    sources, (keep_ref, send_ref, rows) = refs[:4], refs[4:]
    total = sources[0][...].astype(F32)
    for ref in sources[1:]:
        total = total + ref[...].astype(F32)
    rows[...] = total.T
    low = place[1] % 2
    for i in range(4):
        keep = pl.ds(pl.multiple_of((2 * i + low) * 32, 32), 32)
        send = pl.ds(pl.multiple_of((2 * i + 1 - low) * 32, 32), 32)
        keep_ref[i] = rows[keep, :]
        send_ref[i] = rows[send, :].astype(BF)


def add_near(place, parts):
    wide, rows = parts[0].shape
    return pl.pallas_call(
        near_kernel,
        out_shape=(
            jax.ShapeDtypeStruct((4, 32, wide), F32),
            jax.ShapeDtypeStruct((4, 32, wide), BF),
        ),
        in_specs=[SCALARS] + [INSIDE] * 4,
        out_specs=(INSIDE, INSIDE),
        scratch_shapes=[pltpu.VMEM((rows, wide), F32)],
        compiler_params=params(),
        cost_estimate=cost(4 * rows * wide, 2),
        name="add_near",
    )(place, *parts)


def pair_kernel(place, keep_ref, got_ref, *outs):
    for j in range(4):
        at = (place[1] // 2 + j) % 4
        total = keep_ref[at] + got_ref[at].astype(F32)
        outs[j][...] = total.astype(outs[j].dtype)


def add_pair(place, keep, got):
    shape = keep.shape[1:]
    return pl.pallas_call(
        pair_kernel,
        out_shape=tuple(jax.ShapeDtypeStruct(shape, BF if j else F32) for j in range(4)),
        in_specs=[SCALARS, INSIDE, INSIDE],
        out_specs=(INSIDE,) * 4,
        compiler_params=params(),
        cost_estimate=cost(keep.size, 1),
        name="add_pair",
    )(place, keep, got)


def attend_kernel(head_dim, p_hbm, vo_ref, vg_ref, out_hbm, p, out, si, so):
    kv_heads, length, wide = out.shape
    group = wide // head_dim
    incoming = copies_of([(p_hbm.at[pl.ds(g * group, group)], p.at[g]) for g in range(kv_heads)], si)
    outgoing = copies_of([(out.at[g], columns(out_hbm, g, wide)) for g in range(kv_heads)], so)
    start(incoming)
    for g in range(kv_heads):
        own = slice(g * head_dim, (g + 1) * head_dim)
        values = (vo_ref[:, own] + vg_ref[:, own]).astype(BF)
        incoming[g].wait()
        for h in range(group):
            out[g, :, h * head_dim : (h + 1) * head_dim] = lax.dot_general(
                p[g, h], values, (((0,), (0,)), ((), ())), preferred_element_type=F32
            ).astype(BF)
        outgoing[g].start()
    for copy in outgoing:
        copy.wait()


def attend(probability, values_own, values_got, kv_heads):
    heads, length, _ = probability.shape
    head_dim = values_own.shape[1] // kv_heads
    group = heads // kv_heads
    return pl.pallas_call(
        functools.partial(attend_kernel, head_dim),
        out_shape=jax.ShapeDtypeStruct((length, heads * head_dim), BF),
        in_specs=[OUTSIDE, INSIDE, INSIDE],
        out_specs=OUTSIDE,
        scratch_shapes=[
            pltpu.VMEM((kv_heads, group, length, length), BF),
            pltpu.VMEM((kv_heads, length, group * head_dim), BF),
            pltpu.SemaphoreType.DMA((kv_heads,)),
            pltpu.SemaphoreType.DMA((kv_heads,)),
        ],
        compiler_params=params(),
        cost_estimate=cost(2 * heads * head_dim * length * length, 8),
        name="attend",
    )(probability, values_own, values_got)


PLANE = ("y", "xh", "xl")


def exchange(array, axes):
    return lax.all_to_all(array, axes, 0, 0, tiled=True)


def along_z(array, k):
    return lax.ppermute(array, "z", [(z, (z + k) % NZ) for z in range(NZ)])


def gather_near(weight):
    rows, wide = weight.shape
    places = NY * NX
    return exchange(jnp.tile(weight, (places, 1)), PLANE).reshape(places, rows, wide)


def gather_first(near):
    return along_z(near, 1), along_z(near, -1)


def gather_rest(near, up, down, product_part, far_sum):
    pieces = [near, up, down]
    up, down = after(up, product_part), after(down, product_part)
    for _ in range(2):
        up, down = along_z(up, 1), along_z(down, -1)
        pieces += [up, down]
    half = near.shape[0] // 2
    up, down = after(up, far_sum), after(down, far_sum)
    return pieces + [along_z(up[:half], 1), along_z(down[half:], -1)]


def along(array, k, far):
    pairs = []
    for y in range(NY):
        for x in range(NX):
            for c in range(NC):
                ty, tx = ((y + k) % NY, x) if far == (c == 0) else (y, (x + k) % NX)
                for z in range(NZ):
                    source = (((y * 2 + x // 2) * 2 + c) * 2 + x % 2) * NZ + z
                    target = (((ty * 2 + tx // 2) * 2 + c) * 2 + tx % 2) * NZ + z
                    pairs.append((source, target))
    return lax.ppermute(array, AXES, pairs)


def spread(parts, far):
    return [parts[0]] + [along(parts[k], k, far) for k in (1, 2, 3)]


def reduce_last(place, keep, got, attended):
    parts = add_pair(place, keep, got)
    moved = [along_z(parts[j], 2 * j) for j in (1, 2, 3)]
    total = parts[0] + after(moved[0], attended).astype(F32)
    return total + moved[1].astype(F32) + moved[2].astype(F32)


def after(array, other):
    return lax.optimization_barrier((array, other))[0]


def local(activations, queries, keys, segment_ids, cotangent, value_codes, value_scales):
    rows_here, kv_heads = value_scales.shape
    x = lax.axis_index("xh") * 2 + lax.axis_index("xl")
    place = [lax.axis_index("c"), lax.axis_index("z"), lax.axis_index("y"), x]
    place = jnp.stack(place).astype(jnp.int32)
    weight = (
        value_codes.astype(F32).reshape(rows_here, kv_heads, -1) * value_scales[:, :, None]
    ).reshape(rows_here, -1).astype(BF)
    factor = 1.0 / math.sqrt(activations.shape[0] * NY * NX * NC * NZ)
    act_got = swap_cores(other_half(place, activations))
    near = gather_near(weight)
    probability, dvalue = attention_weights(queries, keys, segment_ids, cotangent, kv_heads)
    dv_got = swap_cores(dvalue)
    near = after(near, dv_got)
    up, down = gather_first(near)
    parts = product(place, activations, act_got, dvalue, dv_got, factor)
    far_sums = add_far(place, spread(parts, True))
    pieces = gather_rest(near, up, down, parts[0], far_sums[0])
    keep, send = add_near(place, spread(far_sums, False))
    got = lax.ppermute(send, "z", [(z, z ^ 1) for z in range(NZ)])
    pieces[-1] = after(pieces[-1], send)
    values_own, values_other = partial_values(place, activations, act_got, pieces)
    attended = attend(probability, values_own, swap_cores(values_other), kv_heads)
    return (attended, reduce_last(place, keep, got, attended))


def solution(mesh):
    inner = Mesh(mesh.devices.reshape(NY, 2, NC, 2, NZ), AXES)
    rows = P(AXES, None)
    return jax.shard_map(
        local, mesh=inner, in_specs=(rows,) * 7, out_specs=(rows, rows), check_vma=False
    )
```

```python
import functools
import math

import jax
import jax.numpy as jnp
from jax import lax
from jax.experimental import pallas as pl
from jax.experimental.pallas import tpu as pltpu
from jax.sharding import Mesh, PartitionSpec as P

NY, NX, NC, NZ = 4, 4, 2, 8
AXES = ("y", "xh", "c", "xl", "z")
BF, F32 = jnp.bfloat16, jnp.float32
MIB = 1024 * 1024


def swap_cores(array):
    return lax.ppermute(array, "c", [(0, 1), (1, 0)])


def params(mib=20):
    return pltpu.CompilerParams(vmem_limit_bytes=mib * MIB)


INSIDE = pl.BlockSpec(memory_space=pltpu.VMEM)
OUTSIDE = pl.BlockSpec(memory_space=pl.ANY)
HBM = pl.BlockSpec(memory_space=pltpu.HBM)
SCALARS = pl.BlockSpec(memory_space=pltpu.SMEM)


def copies_of(pairs, sems):
    return [pltpu.make_async_copy(a, b, sems.at[i]) for i, (a, b) in enumerate(pairs)]


def start(copies):
    for copy in copies:
        copy.start()


def columns(ref, i, width):
    return ref.at[:, pl.ds(i * width, width)]


def pick_kernel(place, act_hbm, out_hbm, held, si, so):
    blocks = held.shape[0]
    pairs = []
    for i in range(blocks):
        at = pl.multiple_of(i * 1024 + (1 - place[0]) * 512, 512)
        pairs.append((act_hbm.at[:, pl.ds(at, 512)], held.at[i]))
    incoming = copies_of(pairs, si)
    outgoing = copies_of([(held.at[i], columns(out_hbm, i, 512)) for i in range(blocks)], so)
    start(incoming)
    for i in range(blocks):
        incoming[i].wait()
        outgoing[i].start()
    for copy in outgoing:
        copy.wait()


def other_half(place, activations):
    tokens, width = activations.shape
    blocks = width // 1024
    return pl.pallas_call(
        pick_kernel,
        out_shape=jax.ShapeDtypeStruct((tokens, width // 2), BF),
        in_specs=[SCALARS, HBM],
        out_specs=OUTSIDE,
        scratch_shapes=[
            pltpu.VMEM((blocks, tokens, 512), BF),
            pltpu.SemaphoreType.DMA((blocks,)),
            pltpu.SemaphoreType.DMA((blocks,)),
        ],
        compiler_params=params(60),
        cost_estimate=pl.CostEstimate(flops=0, bytes_accessed=2 * tokens * width, transcendentals=0),
        name="other_half",
    )(place, activations)


def weights_kernel(
    head_dim, q_hbm, k_ref, cot_hbm, segment_ref, p_hbm, dv_ref, q, cot, p, sq, sc, sp
):
    kv_heads, length, wide = q.shape
    group = wide // head_dim
    q_in = copies_of([(columns(q_hbm, g, wide), q.at[g]) for g in range(kv_heads)], sq)
    cot_in = copies_of([(columns(cot_hbm, g, wide), cot.at[g]) for g in range(kv_heads)], sc)
    pairs = [(p.at[g], p_hbm.at[pl.ds(g * group, group)]) for g in range(kv_heads)]
    out = copies_of(pairs, sp)
    for g in range(kv_heads):
        start([q_in[g], cot_in[g]])
    row = segment_ref[...]
    column = jnp.broadcast_to(row.astype(F32), (128, length)).T[:, :1].astype(jnp.int32)
    u = lax.broadcasted_iota(jnp.int32, (length, length), 0)
    t = lax.broadcasted_iota(jnp.int32, (length, length), 1)
    bias = jnp.where((u <= t) & (column == row), 0.0, -1e30)
    rate = math.log2(math.e) / math.sqrt(head_dim)
    for g in range(kv_heads):
        if g < 2:
            for copy in q_in[:1] + cot_in[:1] if g == 0 else q_in[1:] + cot_in[1:]:
                copy.wait()
        total = jnp.zeros((length, head_dim), F32)
        own = slice(g * head_dim, (g + 1) * head_dim)
        for h in range(group):
            cols = slice(h * head_dim, (h + 1) * head_dim)
            scores = lax.dot_general(
                k_ref[:, own], q[g, :, cols], (((1,), (1,)), ((), ())), preferred_element_type=F32
            )
            scores = scores + bias
            highest = jnp.max(scores, axis=0, keepdims=True)
            exponent = jnp.exp2((scores - highest) * rate)
            share = 1.0 / jnp.sum(exponent, axis=0, keepdims=True)
            probability = (exponent * share).astype(BF)
            p[g, h] = probability
            total = total + jnp.dot(probability, cot[g, :, cols], preferred_element_type=F32)
        dv_ref[:, own] = total.astype(BF)
        out[g].start()
    for copy in out:
        copy.wait()


def cost(flops, mib, exps=0):
    return pl.CostEstimate(flops=flops, bytes_accessed=mib * MIB, transcendentals=exps)


def attention_weights(queries, keys, segment_ids, cotangent, kv_heads):
    length, width = queries.shape
    head_dim = keys.shape[1] // kv_heads
    heads = width // head_dim
    return pl.pallas_call(
        functools.partial(weights_kernel, head_dim),
        out_shape=(
            jax.ShapeDtypeStruct((heads, length, length), BF),
            jax.ShapeDtypeStruct(keys.shape, BF),
        ),
        in_specs=[HBM, INSIDE, HBM, INSIDE],
        out_specs=(HBM, INSIDE),
        scratch_shapes=[
            pltpu.VMEM((kv_heads, length, width // kv_heads), BF),
            pltpu.VMEM((kv_heads, length, width // kv_heads), BF),
            pltpu.VMEM((kv_heads, heads // kv_heads, length, length), BF),
        ]
        + [pltpu.SemaphoreType.DMA((kv_heads,))] * 3,
        compiler_params=params(60),
        cost_estimate=cost(4 * width * length * length, 16, heads * length * length),
        name="attention_weights",
    )(queries, keys, cotangent, segment_ids)


def product_kernel(factor, chunks, place, own_ref, got_ref, dvo_ref, dvg_ref, *outs):
    c, y, x = place[0], place[2], place[3]
    dv_own = dvo_ref[...].astype(F32).T.astype(BF)
    dv_got = dvg_ref[...].astype(F32).T.astype(BF)
    for out_ref, k in zip(outs, chunks):
        for m in range(4):
            ty = jnp.where(c == 0, (y + k) % 4, m)
            tx = jnp.where(c == 0, m, (x + k) % 4)
            at_own = pl.multiple_of((ty * 2 + tx // 2) * 1024 + c * 512 + (tx % 2) * 256, 256)
            at_got = pl.multiple_of((ty * 4 + tx) * 256, 256)
            rows = jnp.dot(
                dv_own, own_ref[:, pl.ds(at_own, 256)], preferred_element_type=F32
            ) + jnp.dot(dv_got, got_ref[:, pl.ds(at_got, 256)], preferred_element_type=F32)
            out_ref[m] = (rows * factor).astype(BF)


def product(place, act_own, act_got, dv_own, dv_got, factor, chunks):
    tokens, width = act_own.shape
    wide = dv_own.shape[1]
    return pl.pallas_call(
        functools.partial(product_kernel, factor, chunks),
        out_shape=(jax.ShapeDtypeStruct((4, wide, 256), BF),) * len(chunks),
        in_specs=[SCALARS] + [INSIDE] * 4,
        out_specs=(INSIDE,) * len(chunks),
        compiler_params=params(),
        cost_estimate=cost(tokens * width * wide * len(chunks) // 2, 3 * len(chunks)),
        name="product",
    )(place, act_own, act_got, dv_own, dv_got)


def values_kernel(place, own_ref, got_ref, *refs):
    pieces, (vo_ref, vg_ref, weight, sw) = refs[: NZ + 1], refs[NZ + 1 :]
    rows, wide = pieces[0].shape[1:]
    c = place[0]
    places = weight.shape[0]
    spans = [(0, 0, places), (-1, 0, places), (1, 0, places), (-2, 0, places), (2, 0, places)]
    spans += [(-3, 0, places), (3, 0, places), (4, 0, places // 2), (4, places // 2, places // 2)]
    pairs = []
    for piece, (k, low, count) in zip(pieces, spans):
        z = (place[1] + k + NZ) % NZ
        at = pl.ds(pl.multiple_of(z * rows, rows), rows)
        pairs.append((piece, weight.at[pl.ds(low, count), at]))
    incoming = copies_of(pairs, sw)
    start(incoming)
    for copy in incoming:
        copy.wait()
    own = got = None
    for i in range(places // 2):
        at = pl.multiple_of(i * 1024 + c * 512, 512)
        block = weight[pl.ds(2 * i, 2)].reshape(512, wide)
        left = jnp.dot(own_ref[:, pl.ds(at, 512)], block, preferred_element_type=F32)
        right = jnp.dot(got_ref[:, i * 512 : (i + 1) * 512], block, preferred_element_type=F32)
        own, got = (left, right) if i == 0 else (own + left, got + right)
    vo_ref[...] = own
    vg_ref[...] = got


def partial_values(place, act_own, act_got, pieces):
    tokens, width = act_own.shape
    places, rows, wide = pieces[0].shape
    return pl.pallas_call(
        values_kernel,
        out_shape=(jax.ShapeDtypeStruct((tokens, wide), F32),) * 2,
        in_specs=[SCALARS, INSIDE, INSIDE] + [OUTSIDE] * (1 + NZ),
        out_specs=(INSIDE, INSIDE),
        scratch_shapes=[
            pltpu.VMEM((places, NZ * rows, wide), BF),
            pltpu.SemaphoreType.DMA((NZ + 1,)),
        ],
        compiler_params=params(),
        cost_estimate=cost(2 * tokens * width * wide, 12),
        name="partial_values",
    )(place, act_own, act_got, *pieces)


def add_kernel(place, *refs):
    sources, outs = refs[:4], refs[4:]
    near = jnp.where(place[0] == 0, place[3], place[2])
    for j in (1, 2, 3, 0):
        at = (near + j) % 4
        total = sources[0][at].astype(F32)
        for source in sources[1:]:
            total = total + source[at].astype(F32)
        outs[j][...] = total.astype(BF)


def add_far(place, parts):
    _, wide, rows = parts[0].shape
    return pl.pallas_call(
        add_kernel,
        out_shape=(jax.ShapeDtypeStruct((wide, rows), BF),) * 4,
        in_specs=[SCALARS] + [INSIDE] * 4,
        out_specs=(INSIDE,) * 4,
        compiler_params=params(),
        cost_estimate=cost(16 * rows * wide, 5),
        name="add_far",
    )(place, *parts)


def near_kernel(place, *refs):
    sources, (keep_ref, send_ref, rows) = refs[:4], refs[4:]
    total = sources[0][...].astype(F32)
    for ref in sources[1:]:
        total = total + ref[...].astype(F32)
    rows[...] = total.T
    low = place[1] % 2
    for i in range(4):
        keep = pl.ds(pl.multiple_of((2 * i + low) * 32, 32), 32)
        send = pl.ds(pl.multiple_of((2 * i + 1 - low) * 32, 32), 32)
        keep_ref[i] = rows[keep, :]
        send_ref[i] = rows[send, :].astype(BF)


def add_near(place, parts):
    wide, rows = parts[0].shape
    return pl.pallas_call(
        near_kernel,
        out_shape=(
            jax.ShapeDtypeStruct((4, 32, wide), F32),
            jax.ShapeDtypeStruct((4, 32, wide), BF),
        ),
        in_specs=[SCALARS] + [INSIDE] * 4,
        out_specs=(INSIDE, INSIDE),
        scratch_shapes=[pltpu.VMEM((rows, wide), F32)],
        compiler_params=params(),
        cost_estimate=cost(4 * rows * wide, 2),
        name="add_near",
    )(place, *parts)


def pair_kernel(place, keep_ref, got_ref, *outs):
    for j in range(4):
        at = (place[1] // 2 + j) % 4
        total = keep_ref[at] + got_ref[at].astype(F32)
        outs[j][...] = total.astype(outs[j].dtype)


def add_pair(place, keep, got):
    shape = keep.shape[1:]
    return pl.pallas_call(
        pair_kernel,
        out_shape=tuple(jax.ShapeDtypeStruct(shape, BF if j else F32) for j in range(4)),
        in_specs=[SCALARS, INSIDE, INSIDE],
        out_specs=(INSIDE,) * 4,
        compiler_params=params(),
        cost_estimate=cost(keep.size, 1),
        name="add_pair",
    )(place, keep, got)


def attend_kernel(head_dim, p_hbm, vo_ref, vg_ref, out_hbm, p, out, si, so):
    kv_heads, length, wide = out.shape
    group = wide // head_dim
    incoming = copies_of([(p_hbm.at[pl.ds(g * group, group)], p.at[g]) for g in range(kv_heads)], si)
    outgoing = copies_of([(out.at[g], columns(out_hbm, g, wide)) for g in range(kv_heads)], so)
    start(incoming)
    for g in range(kv_heads):
        own = slice(g * head_dim, (g + 1) * head_dim)
        values = (vo_ref[:, own] + vg_ref[:, own]).astype(BF)
        incoming[g].wait()
        for h in range(group):
            out[g, :, h * head_dim : (h + 1) * head_dim] = lax.dot_general(
                p[g, h], values, (((0,), (0,)), ((), ())), preferred_element_type=F32
            ).astype(BF)
        outgoing[g].start()
    for copy in outgoing:
        copy.wait()


def attend(probability, values_own, values_got, kv_heads):
    heads, length, _ = probability.shape
    head_dim = values_own.shape[1] // kv_heads
    group = heads // kv_heads
    return pl.pallas_call(
        functools.partial(attend_kernel, head_dim),
        out_shape=jax.ShapeDtypeStruct((length, heads * head_dim), BF),
        in_specs=[OUTSIDE, INSIDE, INSIDE],
        out_specs=OUTSIDE,
        scratch_shapes=[
            pltpu.VMEM((kv_heads, group, length, length), BF),
            pltpu.VMEM((kv_heads, length, group * head_dim), BF),
            pltpu.SemaphoreType.DMA((kv_heads,)),
            pltpu.SemaphoreType.DMA((kv_heads,)),
        ],
        compiler_params=params(),
        cost_estimate=cost(2 * heads * head_dim * length * length, 8),
        name="attend",
    )(probability, values_own, values_got)


PLANE = ("y", "xh", "xl")


def exchange(array, axes):
    return lax.all_to_all(array, axes, 0, 0, tiled=True)


def along_z(array, k):
    return lax.ppermute(array, "z", [(z, (z + k) % NZ) for z in range(NZ)])


def gather_near(tiles, shape):
    return exchange(tiles, PLANE).reshape((NY * NX,) + shape)


def ring_step(up, down, other):
    return along_z(after(up, other), 1), along_z(after(down, other), -1)


def along(array, k, far):
    pairs = []
    for y in range(NY):
        for x in range(NX):
            for c in range(NC):
                ty, tx = ((y + k) % NY, x) if far == (c == 0) else (y, (x + k) % NX)
                for z in range(NZ):
                    source = (((y * 2 + x // 2) * 2 + c) * 2 + x % 2) * NZ + z
                    target = (((ty * 2 + tx // 2) * 2 + c) * 2 + tx % 2) * NZ + z
                    pairs.append((source, target))
    return lax.ppermute(array, AXES, pairs)


def spread(parts, far):
    return [parts[0]] + [along(parts[k], k, far) for k in (1, 2, 3)]


def reduce_last(parts, attended):
    moved = [along_z(parts[j], 2 * j) for j in (1, 2, 3)]
    total = parts[0] + after(moved[0], attended).astype(F32)
    return total + moved[1].astype(F32) + moved[2].astype(F32)


def after(array, other):
    return lax.optimization_barrier((array, other))[0]


def local(activations, queries, keys, segment_ids, cotangent, value_codes, value_scales):
    rows_here, kv_heads = value_scales.shape
    x = lax.axis_index("xh") * 2 + lax.axis_index("xl")
    place = [lax.axis_index("c"), lax.axis_index("z"), lax.axis_index("y"), x]
    place = jnp.stack(place).astype(jnp.int32)
    weight = (
        value_codes.astype(F32).reshape(rows_here, kv_heads, -1) * value_scales[:, :, None]
    ).reshape(rows_here, -1).astype(BF)
    factor = 1.0 / math.sqrt(activations.shape[0] * NY * NX * NC * NZ)
    tiles = jnp.tile(weight, (NY * NX, 1))
    act_got = swap_cores(other_half(place, activations))
    near = gather_near(tiles, weight.shape)
    probability, dvalue = attention_weights(queries, keys, segment_ids, cotangent, kv_heads)
    dv_got = swap_cores(dvalue)
    near = after(near, dv_got)
    first = ring_step(near, near, dv_got)
    sides = (place, activations, act_got, dvalue, dv_got, factor)
    away = product(*sides, (1, 2, 3))
    (here,) = product(*sides, (0,))
    second = ring_step(*first, away[0])
    far_sums = add_far(place, [here] + [along(away[k - 1], k, True) for k in (1, 2, 3)])
    keep, send = add_near(place, spread(far_sums, False))
    got = lax.ppermute(send, "z", [(z, z ^ 1) for z in range(NZ)])
    sums = add_pair(place, keep, got)
    third = ring_step(*second, near)
    half = near.shape[0] // 2
    last = ring_step(third[0][:half], third[1][half:], far_sums[0])
    pieces = [near, *first, *second, *third, last[0], after(last[1], sums[1])]
    values_own, values_other = partial_values(place, activations, act_got, pieces)
    attended = attend(probability, values_own, swap_cores(values_other), kv_heads)
    return (attended, reduce_last(sums, attended))


def solution(mesh):
    inner = Mesh(mesh.devices.reshape(NY, 2, NC, 2, NZ), AXES)
    rows = P(AXES, None)
    return jax.shard_map(
        local, mesh=inner, in_specs=(rows,) * 7, out_specs=(rows, rows), check_vma=False
    )
```

```python
import functools
import math

import jax
import jax.numpy as jnp
from jax import lax
from jax.experimental import pallas as pl
from jax.experimental.pallas import tpu as pltpu
from jax.sharding import Mesh, PartitionSpec as P

NY, NX, NC, NZ = 4, 4, 2, 8
AXES = ("y", "xh", "c", "xl", "z")
BF, F32 = jnp.bfloat16, jnp.float32
MIB = 1024 * 1024


def swap_cores(array):
    return lax.ppermute(array, "c", [(0, 1), (1, 0)])


def params(mib=20):
    return pltpu.CompilerParams(vmem_limit_bytes=mib * MIB)


INSIDE = pl.BlockSpec(memory_space=pltpu.VMEM)
OUTSIDE = pl.BlockSpec(memory_space=pl.ANY)
HBM = pl.BlockSpec(memory_space=pltpu.HBM)
SCALARS = pl.BlockSpec(memory_space=pltpu.SMEM)


def copies_of(pairs, sems):
    return [pltpu.make_async_copy(a, b, sems.at[i]) for i, (a, b) in enumerate(pairs)]


def start(copies):
    for copy in copies:
        copy.start()


def columns(ref, i, width):
    return ref.at[:, pl.ds(i * width, width)]


def pick_kernel(place, act_hbm, out_hbm, held, si, so):
    blocks = held.shape[0]
    pairs = []
    for i in range(blocks):
        at = pl.multiple_of(i * 1024 + (1 - place[0]) * 512, 512)
        pairs.append((act_hbm.at[:, pl.ds(at, 512)], held.at[i]))
    incoming = copies_of(pairs, si)
    outgoing = copies_of([(held.at[i], columns(out_hbm, i, 512)) for i in range(blocks)], so)
    start(incoming)
    for i in range(blocks):
        incoming[i].wait()
        outgoing[i].start()
    for copy in outgoing:
        copy.wait()


def other_half(place, activations):
    tokens, width = activations.shape
    blocks = width // 1024
    return pl.pallas_call(
        pick_kernel,
        out_shape=jax.ShapeDtypeStruct((tokens, width // 2), BF),
        in_specs=[SCALARS, HBM],
        out_specs=OUTSIDE,
        scratch_shapes=[
            pltpu.VMEM((blocks, tokens, 512), BF),
            pltpu.SemaphoreType.DMA((blocks,)),
            pltpu.SemaphoreType.DMA((blocks,)),
        ],
        compiler_params=params(60),
        cost_estimate=pl.CostEstimate(flops=0, bytes_accessed=2 * tokens * width, transcendentals=0),
        name="other_half",
    )(place, activations)


def weights_kernel(
    head_dim, q_hbm, k_ref, cot_hbm, segment_ref, p_hbm, dv_ref, q, cot, p, sq, sc, sp
):
    kv_heads, length, wide = q.shape
    group = wide // head_dim
    q_in = copies_of([(columns(q_hbm, g, wide), q.at[g]) for g in range(kv_heads)], sq)
    cot_in = copies_of([(columns(cot_hbm, g, wide), cot.at[g]) for g in range(kv_heads)], sc)
    pairs = [(p.at[g], p_hbm.at[pl.ds(g * group, group)]) for g in range(kv_heads)]
    out = copies_of(pairs, sp)
    for g in range(kv_heads):
        start([q_in[g], cot_in[g]])
    row = segment_ref[...]
    column = jnp.broadcast_to(row.astype(F32), (128, length)).T[:, :1].astype(jnp.int32)
    u = lax.broadcasted_iota(jnp.int32, (length, length), 0)
    t = lax.broadcasted_iota(jnp.int32, (length, length), 1)
    bias = jnp.where((u <= t) & (column == row), 0.0, -1e30)
    rate = math.log2(math.e) / math.sqrt(head_dim)
    for g in range(kv_heads):
        if g < 2:
            for copy in q_in[:1] + cot_in[:1] if g == 0 else q_in[1:] + cot_in[1:]:
                copy.wait()
        total = jnp.zeros((length, head_dim), F32)
        own = slice(g * head_dim, (g + 1) * head_dim)
        for h in range(group):
            cols = slice(h * head_dim, (h + 1) * head_dim)
            scores = lax.dot_general(
                k_ref[:, own], q[g, :, cols], (((1,), (1,)), ((), ())), preferred_element_type=F32
            )
            scores = scores + bias
            highest = jnp.max(scores, axis=0, keepdims=True)
            exponent = jnp.exp2((scores - highest) * rate)
            share = 1.0 / jnp.sum(exponent, axis=0, keepdims=True)
            probability = (exponent * share).astype(BF)
            p[g, h] = probability
            total = total + jnp.dot(probability, cot[g, :, cols], preferred_element_type=F32)
        dv_ref[:, own] = total.astype(BF)
        out[g].start()
    for copy in out:
        copy.wait()


def cost(flops, mib, exps=0):
    return pl.CostEstimate(flops=flops, bytes_accessed=mib * MIB, transcendentals=exps)


def attention_weights(queries, keys, segment_ids, cotangent, kv_heads):
    length, width = queries.shape
    head_dim = keys.shape[1] // kv_heads
    heads = width // head_dim
    return pl.pallas_call(
        functools.partial(weights_kernel, head_dim),
        out_shape=(
            jax.ShapeDtypeStruct((heads, length, length), BF),
            jax.ShapeDtypeStruct(keys.shape, BF),
        ),
        in_specs=[HBM, INSIDE, HBM, INSIDE],
        out_specs=(HBM, INSIDE),
        scratch_shapes=[
            pltpu.VMEM((kv_heads, length, width // kv_heads), BF),
            pltpu.VMEM((kv_heads, length, width // kv_heads), BF),
            pltpu.VMEM((kv_heads, heads // kv_heads, length, length), BF),
        ]
        + [pltpu.SemaphoreType.DMA((kv_heads,))] * 3,
        compiler_params=params(60),
        cost_estimate=cost(4 * width * length * length, 16, heads * length * length),
        name="attention_weights",
    )(queries, keys, cotangent, segment_ids)


def product_kernel(factor, chunks, place, own_ref, got_ref, dvo_ref, dvg_ref, *outs):
    c, y, x = place[0], place[2], place[3]
    dv_own = dvo_ref[...].astype(F32).T.astype(BF)
    dv_got = dvg_ref[...].astype(F32).T.astype(BF)
    for out_ref, k in zip(outs, chunks):
        for m in range(4):
            ty = jnp.where(c == 0, (y + k) % 4, m)
            tx = jnp.where(c == 0, m, (x + k) % 4)
            at_own = pl.multiple_of((ty * 2 + tx // 2) * 1024 + c * 512 + (tx % 2) * 256, 256)
            at_got = pl.multiple_of((ty * 4 + tx) * 256, 256)
            rows = jnp.dot(
                dv_own, own_ref[:, pl.ds(at_own, 256)], preferred_element_type=F32
            ) + jnp.dot(dv_got, got_ref[:, pl.ds(at_got, 256)], preferred_element_type=F32)
            out_ref[m] = (rows * factor).astype(BF)


def product(place, act_own, act_got, dv_own, dv_got, factor, chunks):
    tokens, width = act_own.shape
    wide = dv_own.shape[1]
    return pl.pallas_call(
        functools.partial(product_kernel, factor, chunks),
        out_shape=(jax.ShapeDtypeStruct((4, wide, 256), BF),) * len(chunks),
        in_specs=[SCALARS] + [INSIDE] * 4,
        out_specs=(INSIDE,) * len(chunks),
        compiler_params=params(),
        cost_estimate=cost(tokens * width * wide * len(chunks) // 2, 3 * len(chunks)),
        name="product",
    )(place, act_own, act_got, dv_own, dv_got)


def values_kernel(place, own_ref, got_ref, *refs):
    pieces, (vo_ref, vg_ref, weight, sw) = refs[: NZ + 1], refs[NZ + 1 :]
    rows, wide = pieces[0].shape[1:]
    c = place[0]
    places = weight.shape[0]
    sign = 1 - 2 * (place[1] % 2)
    spans = [(0, 0, places)]
    for k in (1, 2, 3):
        spans += [(k, 0, places), (-k, 0, places)]
    spans += [(4, 0, places // 2), (4, places // 2, places // 2)]
    pairs = []
    for piece, (k, low, count) in zip(pieces, spans):
        z = (place[1] + sign * k + NZ) % NZ
        at = pl.ds(pl.multiple_of(z * rows, rows), rows)
        pairs.append((piece, weight.at[pl.ds(low, count), at]))
    incoming = copies_of(pairs, sw)
    start(incoming)
    for copy in incoming:
        copy.wait()
    own = got = None
    for i in range(places // 2):
        at = pl.multiple_of(i * 1024 + c * 512, 512)
        block = weight[pl.ds(2 * i, 2)].reshape(512, wide)
        left = jnp.dot(own_ref[:, pl.ds(at, 512)], block, preferred_element_type=F32)
        right = jnp.dot(got_ref[:, i * 512 : (i + 1) * 512], block, preferred_element_type=F32)
        own, got = (left, right) if i == 0 else (own + left, got + right)
    vo_ref[...] = own
    vg_ref[...] = got


def partial_values(place, act_own, act_got, pieces):
    tokens, width = act_own.shape
    places, rows, wide = pieces[0].shape
    return pl.pallas_call(
        values_kernel,
        out_shape=(jax.ShapeDtypeStruct((tokens, wide), F32),) * 2,
        in_specs=[SCALARS, INSIDE, INSIDE] + [OUTSIDE] * (1 + NZ),
        out_specs=(INSIDE, INSIDE),
        scratch_shapes=[
            pltpu.VMEM((places, NZ * rows, wide), BF),
            pltpu.SemaphoreType.DMA((NZ + 1,)),
        ],
        compiler_params=params(),
        cost_estimate=cost(2 * tokens * width * wide, 12),
        name="partial_values",
    )(place, act_own, act_got, *pieces)


def add_kernel(place, *refs):
    sources, outs = refs[:4], refs[4:]
    near = jnp.where(place[0] == 0, place[3], place[2])
    for j in (1, 2, 3, 0):
        at = (near + j) % 4
        total = sources[0][at].astype(F32)
        for source in sources[1:]:
            total = total + source[at].astype(F32)
        outs[j][...] = total.astype(BF)


def add_far(place, parts):
    _, wide, rows = parts[0].shape
    return pl.pallas_call(
        add_kernel,
        out_shape=(jax.ShapeDtypeStruct((wide, rows), BF),) * 4,
        in_specs=[SCALARS] + [INSIDE] * 4,
        out_specs=(INSIDE,) * 4,
        compiler_params=params(),
        cost_estimate=cost(16 * rows * wide, 5),
        name="add_far",
    )(place, *parts)


def near_kernel(place, *refs):
    sources, (keep_ref, send_ref, rows) = refs[:4], refs[4:]
    total = sources[0][...].astype(F32)
    for ref in sources[1:]:
        total = total + ref[...].astype(F32)
    rows[...] = total.T
    low = place[1] % 2
    for i in range(4):
        keep = pl.ds(pl.multiple_of((2 * i + low) * 32, 32), 32)
        send = pl.ds(pl.multiple_of((2 * i + 1 - low) * 32, 32), 32)
        keep_ref[i] = rows[keep, :]
        send_ref[i] = rows[send, :].astype(BF)


def add_near(place, parts):
    wide, rows = parts[0].shape
    return pl.pallas_call(
        near_kernel,
        out_shape=(
            jax.ShapeDtypeStruct((4, 32, wide), F32),
            jax.ShapeDtypeStruct((4, 32, wide), BF),
        ),
        in_specs=[SCALARS] + [INSIDE] * 4,
        out_specs=(INSIDE, INSIDE),
        scratch_shapes=[pltpu.VMEM((rows, wide), F32)],
        compiler_params=params(),
        cost_estimate=cost(4 * rows * wide, 2),
        name="add_near",
    )(place, *parts)


def pair_kernel(place, keep_ref, got_ref, *outs):
    for j in range(4):
        at = (place[1] // 2) ^ j
        total = keep_ref[at] + got_ref[at].astype(F32)
        outs[j][...] = total.astype(outs[j].dtype)


def add_pair(place, keep, got):
    shape = keep.shape[1:]
    return pl.pallas_call(
        pair_kernel,
        out_shape=tuple(jax.ShapeDtypeStruct(shape, BF if j else F32) for j in range(4)),
        in_specs=[SCALARS, INSIDE, INSIDE],
        out_specs=(INSIDE,) * 4,
        compiler_params=params(),
        cost_estimate=cost(keep.size, 1),
        name="add_pair",
    )(place, keep, got)


def attend_kernel(head_dim, p_hbm, vo_ref, vg_ref, out_hbm, p, out, si, so):
    kv_heads, length, wide = out.shape
    group = wide // head_dim
    incoming = copies_of([(p_hbm.at[pl.ds(g * group, group)], p.at[g]) for g in range(kv_heads)], si)
    outgoing = copies_of([(out.at[g], columns(out_hbm, g, wide)) for g in range(kv_heads)], so)
    start(incoming)
    for g in range(kv_heads):
        own = slice(g * head_dim, (g + 1) * head_dim)
        values = (vo_ref[:, own] + vg_ref[:, own]).astype(BF)
        incoming[g].wait()
        for h in range(group):
            out[g, :, h * head_dim : (h + 1) * head_dim] = lax.dot_general(
                p[g, h], values, (((0,), (0,)), ((), ())), preferred_element_type=F32
            ).astype(BF)
        outgoing[g].start()
    for copy in outgoing:
        copy.wait()


def attend(probability, values_own, values_got, kv_heads):
    heads, length, _ = probability.shape
    head_dim = values_own.shape[1] // kv_heads
    group = heads // kv_heads
    return pl.pallas_call(
        functools.partial(attend_kernel, head_dim),
        out_shape=jax.ShapeDtypeStruct((length, heads * head_dim), BF),
        in_specs=[OUTSIDE, INSIDE, INSIDE],
        out_specs=OUTSIDE,
        scratch_shapes=[
            pltpu.VMEM((kv_heads, group, length, length), BF),
            pltpu.VMEM((kv_heads, length, group * head_dim), BF),
            pltpu.SemaphoreType.DMA((kv_heads,)),
            pltpu.SemaphoreType.DMA((kv_heads,)),
        ],
        compiler_params=params(),
        cost_estimate=cost(2 * heads * head_dim * length * length, 8),
        name="attend",
    )(probability, values_own, values_got)


PLANE = ("y", "xh", "xl")


def exchange(array, axes):
    return lax.all_to_all(array, axes, 0, 0, tiled=True)


def pair_z(array, distance):
    return lax.ppermute(array, "z", [(z, z ^ distance) for z in range(NZ)])


def pair_odd(array):
    return lax.ppermute(array, "z", [(z, (((z + 1) ^ 1) - 1) % NZ) for z in range(NZ)])


def gather_near(tiles, shape):
    return exchange(tiles, PLANE).reshape((NY * NX,) + shape)


def ring_step(even, odd, other):
    return pair_z(after(odd, other), 1), pair_odd(after(even, other))


def along(array, k, far):
    pairs = []
    for y in range(NY):
        for x in range(NX):
            for c in range(NC):
                ty, tx = ((y + k) % NY, x) if far == (c == 0) else (y, (x + k) % NX)
                for z in range(NZ):
                    source = (((y * 2 + x // 2) * 2 + c) * 2 + x % 2) * NZ + z
                    target = (((ty * 2 + tx // 2) * 2 + c) * 2 + tx % 2) * NZ + z
                    pairs.append((source, target))
    return lax.ppermute(array, AXES, pairs)


def spread(parts, far):
    return [parts[0]] + [along(parts[k], k, far) for k in (1, 2, 3)]


def reduce_last(parts, attended):
    moved = [pair_z(parts[j], 2 * j) for j in (1, 2, 3)]
    total = parts[0] + after(moved[0], attended).astype(F32)
    return total + moved[1].astype(F32) + moved[2].astype(F32)


def after(array, other):
    return lax.optimization_barrier((array, other))[0]


def local(activations, queries, keys, segment_ids, cotangent, value_codes, value_scales):
    rows_here, kv_heads = value_scales.shape
    x = lax.axis_index("xh") * 2 + lax.axis_index("xl")
    place = [lax.axis_index("c"), lax.axis_index("z"), lax.axis_index("y"), x]
    place = jnp.stack(place).astype(jnp.int32)
    weight = (
        value_codes.astype(F32).reshape(rows_here, kv_heads, -1) * value_scales[:, :, None]
    ).reshape(rows_here, -1).astype(BF)
    factor = 1.0 / math.sqrt(activations.shape[0] * NY * NX * NC * NZ)
    tiles = jnp.tile(weight, (NY * NX, 1))
    act_got = swap_cores(other_half(place, activations))
    near = gather_near(tiles, weight.shape)
    probability, dvalue = attention_weights(queries, keys, segment_ids, cotangent, kv_heads)
    dv_got = swap_cores(dvalue)
    near = after(near, dv_got)
    first = ring_step(near, near, dv_got)
    sides = (place, activations, act_got, dvalue, dv_got, factor)
    away = product(*sides, (1, 2, 3))
    (here,) = product(*sides, (0,))
    second = ring_step(*first, away[0])
    far_sums = add_far(place, [here] + [along(away[k - 1], k, True) for k in (1, 2, 3)])
    keep, send = add_near(place, spread(far_sums, False))
    got = pair_z(send, 1)
    sums = add_pair(place, keep, got)
    third = ring_step(*second, near)
    half = near.shape[0] // 2
    last = ring_step(third[0][half:], third[1][:half], far_sums[0])
    pieces = [near, *first, *second, *third, last[0], after(last[1], sums[1])]
    values_own, values_other = partial_values(place, activations, act_got, pieces)
    attended = attend(probability, values_own, swap_cores(values_other), kv_heads)
    return (attended, reduce_last(sums, attended))


def solution(mesh):
    inner = Mesh(mesh.devices.reshape(NY, 2, NC, 2, NZ), AXES)
    rows = P(AXES, None)
    return jax.shard_map(
        local, mesh=inner, in_specs=(rows,) * 7, out_specs=(rows, rows), check_vma=False
    )
```
